128 devices in a mesh: gx: 8 (over x_hi, z), gy: 16 (over y, x_lo, core).
Axes of the slice: x: 4 (x_hi: 2, x_lo: 2; x = x_hi * 2 + x_lo), y: 4, z: 4, core: 2. Of those that a mesh axis runs over, the one named last changes fastest.
Arguments:
- die_basis: float32 [128, 512, 512], P('gx', 'gy'), may hold values from -0.0390625 to 0.0390625
- die_coeff: float32 [5, 128, 512], P(None, 'gx', 'gy'), may hold values from 0.2 to 5
- pkg_basis: float32 [4096, 64, 512], P(('gx', 'gy')), may hold values from -0.09375 to 0.09375
- send_blocks: int32 [128, 4, 4], P(('gx', 'gy')), may hold values from 0 to 31
- columns: int32 [5, 4096, 4], P(None, ('gx', 'gy')), may hold values from 0 to 47
- counts: int32 [5, 4096], P(None, ('gx', 'gy')), may hold values from 1 to 4
- pkg_blocks: float32 [5, 4096, 64, 256], P(None, ('gx', 'gy')), may hold values from -48 to 48
Outputs:
- reduced: float32 [5, 512, 512], replicated
The draws below stay inside these ranges and needn't reach their ends.
Inputs may be any that keep to these rules, and one draw needn't show every extreme that they name: `columns`: indices below 32 name the partition's own blocks, the others its ghost blocks in the order of the statement.
All inputs are finite; a program needn't handle non-finite values.
Results may differ from the reference program's by a relative error of at most 0.0001.
Values sent between devices are 32-bit elements; how exact they have to be, the bound alone decides.
A program may use at most 256 MiB of HBM per device.

```python
import math
import jax
import jax.numpy as jnp
from jax import lax

K = 512
TERMS = 5
BLK = 64
NB = 4
GCAP = 4
PB = 32
NDEV = 128
NX = 128
NY = 512
NPB = 4096
N_GX = 8
N_GY = 16


def touch_ends(result, key, least, largest):
    place = [jax.random.randint(jax.random.fold_in(key, axis), (), 0, length) for axis, length in enumerate(result.shape)]
    main_axis = result.shape.index(max(result.shape))
    neighbour = place[:main_axis] + [(place[main_axis] + 1) % result.shape[main_axis]] + place[main_axis + 1:]
    return result.at[tuple(place)].set(least).at[tuple(neighbour)].set(largest)


def spiked(values, own_key, source, target, parts, factor):
    def block_of(axis_at):
        return (jnp.arange(values.shape[axis_at]) // (values.shape[axis_at] // parts)).reshape((-1,) + (1,) * (values.ndim - 1 - axis_at))

    one_side = jax.random.permutation(own_key, parts)[block_of(target)]
    second = (block_of(target) + parts // 2) % parts
    return jnp.where((block_of(source) == one_side) | (block_of(source) == second), factor * values, values)


def shard_levels(stream_key, dims, pieces, smallest, high):
    factor_of = 1.0
    for dim, parts in pieces:
        heights = jax.random.uniform(jax.random.fold_in(jax.random.fold_in(stream_key, 6), dim), (parts,), jnp.float32, smallest / len(pieces), high / len(pieces))
        factor_of = factor_of * jnp.repeat(jnp.exp(heights), dims[dim] // parts).reshape((-1,) + (1,) * (len(dims) - 1 - dim))
    return factor_of


def normal_values(key, dims, scale, most, cuts=(), kind=jnp.bfloat16):
    result = scale * jax.random.normal(key, dims, jnp.float32)
    if cuts:
        result = result * shard_levels(key, dims, cuts, -0.22, 0.18)
    return jnp.clip(result, -most, most).astype(kind)


def gaussian_with(stream_key, extent, deviation, limit, cuts, heavy, held_as=jnp.bfloat16):
    array = deviation * jax.random.normal(stream_key, extent, jnp.float32)
    if cuts:
        array = array * shard_levels(stream_key, extent, cuts, -0.22, 0.18)
    return jnp.clip(spiked(array, jax.random.fold_in(stream_key, 3), *heavy), -limit, limit).astype(held_as)


def setup_inputs(seed: int = 0) -> dict:
    keys = jax.random.split(jax.random.key(seed), 8)
    return {
        "die_basis": gaussian_with(keys[0], (NX, NY, K), ((NX * NY + NPB * BLK) ** -0.5), 0.0390625, ((0, 8), (1, 16)), (0, 2, 8, 2.0), jnp.float32),
        "die_coeff": jnp.clip(jnp.exp(math.log(5.0) - 3.218876 * jax.random.uniform(keys[1], (TERMS, NX, NY), jnp.float32) ** shard_levels(keys[1], (TERMS, NX, NY), ((1, 8), (2, 16)), -0.2, 0.2)), 0.2, 5.0),
        "pkg_basis": gaussian_with(keys[2], (NPB, BLK, K), ((NX * NY + NPB * BLK) ** -0.5), 0.09375, ((0, 128),), (0, 2, 128, 5.5), jnp.float32),
        "send_blocks": touch_ends(jax.random.randint(keys[3], (NDEV, 4, GCAP), 0, PB), jax.random.fold_in(keys[3], 1), 0, PB - 1).astype(jnp.int32),
        "columns": touch_ends(jax.random.randint(keys[4], (TERMS, NPB, NB), 0, PB + 4 * GCAP), jax.random.fold_in(keys[4], 1), 0, (PB + 4 * GCAP) - 1).astype(jnp.int32),
        "counts": touch_ends(jax.random.randint(keys[5], (TERMS, NPB), 1, NB + 1), jax.random.fold_in(keys[5], 1), 1, NB).astype(jnp.int32),
        "pkg_blocks": normal_values(keys[6], (TERMS, NPB, BLK, NB * BLK), 8.0, 48.0, ((1, 128),), jnp.float32),
    }


highest = lax.Precision.HIGHEST


def weighted_gram(weights, field):
    width = field.shape[-1]
    flat = field.reshape(-1, width)
    scaled = weights.reshape(-1, 1) * flat
    return lax.dot_general(flat, scaled, (((0,), (0,)), ((), ())), precision=highest, preferred_element_type=jnp.float32)


def die_terms(basis, coeff, next_x_row, next_y_col):
    next_x = jnp.concatenate([basis[1:], next_x_row], axis=0)
    next_y = jnp.concatenate([basis[:, 1:], next_y_col], axis=1)
    diff_x = basis - next_x
    diff_y = basis - next_y
    return jnp.stack([
        weighted_gram(coeff[0], basis),
        weighted_gram(coeff[1], diff_x),
        weighted_gram(coeff[2], diff_y),
        weighted_gram(coeff[3], basis),
        weighted_gram(coeff[4], diff_x) + weighted_gram(coeff[4], diff_y),
    ])


def package_terms(owned, table, columns, counts, blocks):
    row_count = owned.shape[0]
    block = owned.shape[1]
    width = owned.shape[2]
    entries = columns.shape[-1]
    results = []
    for term_idx in range(columns.shape[0]):
        picked = table[columns[term_idx]]
        live = (jnp.arange(entries, dtype=jnp.int32)[None, :] < counts[term_idx][:, None]).astype(jnp.float32)
        matrices = blocks[term_idx].reshape(row_count, block, entries, block) * live[:, None, :, None]
        image = jnp.einsum("rinj,rnjk->rik", matrices, picked, precision=highest)
        results.append(lax.dot_general(owned.reshape(-1, width), image.reshape(-1, width), (((0,), (0,)), ((), ())), precision=highest, preferred_element_type=jnp.float32))
    return jnp.stack(results)


def reference(die_basis, die_coeff, pkg_basis, send_blocks, columns, counts, pkg_blocks):
    zero_row = jnp.zeros((1, NY, K), jnp.float32)
    zero_col = jnp.zeros((NX, 1, K), jnp.float32)
    total = die_terms(die_basis, die_coeff, zero_row, zero_col)

    def local_blocks(source_dev):
        return lax.dynamic_slice_in_dim(pkg_basis, (source_dev * PB).astype(jnp.int32), PB, 0)

    def device_term(dev_idx, accum):
        dev_idx = jnp.asarray(dev_idx).astype(jnp.int32)
        row_a = dev_idx // N_GY
        col_b = dev_idx % N_GY
        sources = [((row_a - 1) % N_GX) * N_GY + col_b, ((row_a + 1) % N_GX) * N_GY + col_b,
                   row_a * N_GY + (col_b - 1) % N_GY, row_a * N_GY + (col_b + 1) % N_GY]
        ghosts = []
        for direction, source_dev in enumerate(sources):
            lists = lax.dynamic_index_in_dim(send_blocks, source_dev.astype(jnp.int32), 0, keepdims=False)
            ghosts.append(local_blocks(source_dev)[lists[direction]])
        owned = local_blocks(dev_idx)
        table = jnp.concatenate([owned] + ghosts, axis=0)
        start = (dev_idx * PB).astype(jnp.int32)
        dev_columns = lax.dynamic_slice_in_dim(columns, start, PB, 1)
        dev_counts = lax.dynamic_slice_in_dim(counts, start, PB, 1)
        dev_blocks = lax.dynamic_slice_in_dim(pkg_blocks, start, PB, 1)
        return accum + package_terms(owned, table, dev_columns, dev_counts, dev_blocks)

    return lax.fori_loop(0, NDEV, device_term, total)
```

```python
import jax
import jax.numpy as jnp
from jax import lax
from jax.experimental import pallas as pl
from jax.experimental.pallas import tpu as pltpu
from jax.sharding import PartitionSpec as P

MESH = pl.DeviceIdType.MESH
f32 = jnp.float32
bf16 = jnp.bfloat16
TERMS = 5
HALF = 1024
SHARE = (256, 64, 16)


def split(value):
    high = value.astype(bf16)
    low = (value - high.astype(f32)).astype(bf16)
    return high, low


def dot3(left, right):
    return jnp.dot(
        jnp.concatenate([left[0], left[1], left[0]], axis=1),
        jnp.concatenate([right[0], right[0], right[1]], axis=0),
        preferred_element_type=f32,
    )


def kernel(
    die, coeff, basis, lists, columns, counts, blocks, out,
    table, basis_t, staged, image, total, field_t, field, share, summed,
    ghost_out, ghost_in, row_in, col_out, col_in, got_core, got_0, got_1, got_2,
    ghost_send, ghost_recv, halo_send, halo_recv, stage_sem, out_sem, send_sem, recv_sem,
):
    gx, gy = lax.axis_index("gx"), lax.axis_index("gy")
    core = lax.rem(gy, 2)
    spot = ((gx // 4) * 2 + lax.rem(gy // 2, 2), gy // 4, lax.rem(gx, 4))
    got = (got_0, got_1, got_2)

    def device_at(x, y, z, on_core):
        return ((x // 2) * 4 + z, y * 4 + lax.rem(x, 2) * 2 + on_core)

    def which(axis):
        return ((2 - axis) * (1 - axis) // 2, axis * (2 - axis), axis * (axis - 1) // 2)

    def along(axis, steps):
        x, y, z = (lax.rem(s + steps * w, 4) for s, w in zip(spot, which(axis)))
        return device_at(x, y, z, core)

    def place_on(axis):
        return sum(s * w for s, w in zip(spot, which(axis)))

    sibling = device_at(*spot, 1 - core)
    around = (
        (lax.rem(gx + 1, 8), gy),
        (lax.rem(gx + 7, 8), gy),
        (gx, lax.rem(gy + 1, 16)),
        (gx, lax.rem(gy + 15, 16)),
    )

    def stage_copy(half_term, slot):
        term, half = half_term // 2, lax.rem(half_term, 2)
        return pltpu.make_async_copy(
            blocks.at[term, pl.ds(half * 16, 16)], staged.at[slot], stage_sem.at[slot]
        )

    stage_copy(0, 0).start()

    barrier = pltpu.get_barrier_semaphore()
    partners = [along(axis, steps) for axis in range(3) for steps in (1, 2, 3)]
    partners += [sibling, *around]
    for partner in partners:
        pl.semaphore_signal(barrier, inc=1, device_id=partner, device_id_type=MESH)
    pl.semaphore_wait(barrier, len(partners))

    def remote(source, target, send, recv, device):
        return pltpu.make_async_remote_copy(
            src_ref=source, dst_ref=target, send_sem=send, recv_sem=recv,
            device_id=device, device_id_type=MESH,
        )

    row_copy = remote(die.at[0], row_in, halo_send.at[0], halo_recv.at[0], around[1])
    row_copy.start()
    col_out[...] = die[:, 0, :]
    col_copy = remote(col_out, col_in, halo_send.at[1], halo_recv.at[1], around[3])
    col_copy.start()
    ghost_copies = []
    for side in range(4):
        for slot in range(4):
            ghost_out[side, slot] = basis[lists[0, side, slot]]
        copy = remote(
            ghost_out.at[side], ghost_in.at[side], ghost_send.at[side], ghost_recv.at[side],
            around[side],
        )
        copy.start()
        ghost_copies.append(copy)

    def prepare(group, carry):
        value = basis[pl.ds(group * 4, 4)].reshape(256, 512)
        high, low = split(value)
        table[0, pl.ds(group * 4, 4)] = high.reshape(4, 64, 512)
        table[1, pl.ds(group * 4, 4)] = low.reshape(4, 64, 512)
        high, low = split(value.T)
        basis_t[group, 0] = high
        basis_t[group, 1] = low
        return carry

    lax.fori_loop(0, 8, prepare, 0)

    own = die[...]
    row_copy.wait()
    col_copy.wait()
    next_row = jnp.where(gx == 7, 0.0, row_in[...])
    next_col = jnp.where(gy == 15, 0.0, col_in[...])

    def keep_field(index, value):
        flat = value.reshape(512, 512)
        high, low = split(flat)
        field[index, 0] = high
        field[index, 1] = low
        field_t[index] = flat.T

    keep_field(0, own)
    keep_field(1, own - jnp.concatenate([own[1:], next_row[None]], axis=0))
    last = lax.broadcasted_iota(jnp.int32, (16, 32, 512), 1) == 31
    keep_field(2, own - jnp.where(last, next_col[:, None, :], jnp.roll(own, -1, axis=1)))
    share[...] = jnp.zeros_like(share)

    def die_term(step, carry):
        index = step // 2
        odd = lax.rem(step, 2)
        term = (1 - odd) * index + odd * (3 + (index + 1) // 2)
        weighted = split(field_t[index] * coeff[pl.ds(term, 1), :])
        gram = dot3(weighted, (field[index, 0], field[index, 1]))
        for lane in range(4):
            share[term, lane * 512 : (lane + 1) * 512] += gram[:, lane * 128 : (lane + 1) * 128]
        return carry

    lax.fori_loop(0, 6, die_term, 0)

    for side in range(4):
        ghost_copies[side].wait()
        high, low = split(ghost_in[side])
        table[0, 32 + side * 4 : 36 + side * 4] = high
        table[1, 32 + side * 4 : 36 + side * 4] = low

    lane_at = lax.broadcasted_iota(jnp.int32, (64, 256), 1)

    def half_term(at):
        term, half, slot = at // 2, lax.rem(at, 2), lax.rem(at, 2)
        stage_copy(at, slot).wait()

        @pl.when(at < 2 * TERMS - 1)
        def _():
            stage_copy(at + 1, 1 - slot).start()

        for step in range(16):
            row = half * 16 + step
            kept = jnp.where(lane_at < counts[term, row] * 64, staged[slot, step], 0.0)
            high, low = split(kept)
            picks = [columns[term, row, entry] for entry in range(4)]
            picked_high = jnp.concatenate([table[0, pick] for pick in picks], axis=0)
            picked_low = jnp.concatenate([table[1, pick] for pick in picks], axis=0)
            both = jnp.dot(
                jnp.concatenate([high, low], axis=0), picked_high, preferred_element_type=f32
            )
            value = both[:64] + both[64:] + jnp.dot(high, picked_low, preferred_element_type=f32)
            high, low = split(value)
            image[0, step * 64 : (step + 1) * 64] = high
            image[1, step * 64 : (step + 1) * 64] = low
        highs = [basis_t[half * 4 + part, 0] for part in range(4)]
        lows = [basis_t[half * 4 + part, 1] for part in range(4)]
        product = jnp.dot(
            jnp.concatenate(highs + lows + highs, axis=1),
            jnp.concatenate([image[0], image[0], image[1]], axis=0),
            preferred_element_type=f32,
        )
        for lane in range(4):
            share[term, lane * 512 : (lane + 1) * 512] += product[:, lane * 128 : (lane + 1) * 128]

    def offset(term, level):
        start = core * HALF
        for i in range(level):
            start = start + place_on(lax.rem(term + i, 3)) * SHARE[i]
        return pl.multiple_of(start, 16)

    def wait_bytes(ref, sem):
        pltpu.make_async_copy(ref, ref, sem).wait()

    def core_send(term):
        there = pl.multiple_of((1 - core) * HALF, 16)
        remote(
            share.at[term, pl.ds(there, HALF)], got_core.at[term],
            send_sem.at[term, 0], recv_sem.at[term, 0], sibling,
        ).start()

    def core_add(term):
        wait_bytes(got_core.at[term], recv_sem.at[term, 0])
        share[term, pl.ds(offset(term, 0), HALF)] += got_core[term]

    def scatter(term, level):
        axis, base, rows = lax.rem(term + level, 3), offset(term, level), SHARE[level]
        for steps in (1, 2, 3):
            there = pl.multiple_of(base + lax.rem(place_on(axis) + steps, 4) * rows, 16)
            remote(
                share.at[term, pl.ds(there, rows)],
                got[level].at[term, pl.ds((steps - 1) * rows, rows)],
                send_sem.at[term, 1 + level], recv_sem.at[term, 1 + level], along(axis, steps),
            ).start()

    def add(term, level, target):
        wait_bytes(got[level].at[term], recv_sem.at[term, 1 + level])
        rows, here = SHARE[level], pl.ds(offset(term, level + 1), SHARE[level])
        target[term, here] = (
            share[term, here]
            + got[level][term, :rows]
            + got[level][term, rows : 2 * rows]
            + got[level][term, 2 * rows :]
        )

    def gather(term, level):
        here = pl.ds(offset(term, level + 1), SHARE[level])
        axis = lax.rem(term + level, 3)
        for steps in (1, 2, 3):
            remote(
                summed.at[term, here], summed.at[term, here],
                send_sem.at[term, 4 + level], recv_sem.at[term, 4 + level], along(axis, steps),
            ).start()

    def gathered(term, level):
        wait_bytes(got[level].at[term], recv_sem.at[term, 4 + level])

    def core_gather(term):
        here = pl.ds(offset(term, 0), HALF)
        remote(
            summed.at[term, here], summed.at[term, here],
            send_sem.at[term, 7], recv_sem.at[term, 7], sibling,
        ).start()

    def write(term):
        wait_bytes(got_core.at[term], recv_sem.at[term, 7])
        for lane in range(4):
            pltpu.make_async_copy(
                summed.at[term, pl.ds(lane * 512, 512)],
                out.at[term, :, pl.ds(lane * 128, 128)],
                out_sem.at[term],
            ).start()

    def stage_0(term):
        core_send(term)

    def stage_1(term):
        core_add(term)
        scatter(term, 0)

    def stage_2(term):
        add(term, 0, share)
        scatter(term, 1)

    def stage_3(term):
        add(term, 1, share)
        scatter(term, 2)

    def stage_4(term):
        add(term, 2, summed)
        gather(term, 2)

    def stage_5(term):
        gathered(term, 2)
        gather(term, 1)

    def stage_6(term):
        gathered(term, 1)
        gather(term, 0)

    def stage_7(term):
        gathered(term, 0)
        core_gather(term)

    stages = (stage_0, stage_1, stage_2, stage_3, stage_4, stage_5, stage_6, stage_7, write)

    def turn(at, carry):
        @pl.when(at < 2 * TERMS)
        def _():
            half_term(at)

        for k in reversed(range(len(stages))):
            since = at - 1 - k
            term = since // 2

            @pl.when((since >= 0) & (since < 2 * TERMS) & (lax.rem(since + 20, 2) == 0))
            def _(k=k, term=term):
                stages[k](term)

        return carry

    lax.fori_loop(0, 2 * TERMS + 8, turn, 0)

    def finish(term, carry):
        for k in (0, 7):
            wait_bytes(got_core.at[term], send_sem.at[term, k])
        for level in range(3):
            wait_bytes(got[level].at[term], send_sem.at[term, 1 + level])
            wait_bytes(got[level].at[term], send_sem.at[term, 4 + level])
        wait_bytes(summed.at[term], out_sem.at[term])
        return carry

    lax.fori_loop(0, TERMS, finish, 0)


def body(die_basis, die_coeff, pkg_basis, send_blocks, columns, counts, pkg_blocks):
    vmem = pl.BlockSpec(memory_space=pltpu.VMEM)
    smem = pl.BlockSpec(memory_space=pltpu.SMEM)
    anywhere = pl.BlockSpec(memory_space=pl.ANY)
    dma = pltpu.SemaphoreType.DMA
    return pl.pallas_call(
        kernel,
        out_shape=jax.ShapeDtypeStruct((TERMS, 512, 512), f32),
        in_specs=[vmem, vmem, vmem, smem, smem, smem, anywhere],
        out_specs=anywhere,
        scratch_shapes=[
            pltpu.VMEM((2, 48, 64, 512), bf16),
            pltpu.VMEM((8, 2, 512, 256), bf16),
            pltpu.VMEM((2, 16, 64, 256), f32),
            pltpu.VMEM((2, 1024, 512), bf16),
            pltpu.VMEM((8, 128), f32),
            pltpu.VMEM((3, 512, 512), f32),
            pltpu.VMEM((3, 2, 512, 512), bf16),
            pltpu.VMEM((TERMS, 2 * HALF, 128), f32),
            pltpu.VMEM((TERMS, 2 * HALF, 128), f32),
            pltpu.VMEM((4, 4, 64, 512), f32),
            pltpu.VMEM((4, 4, 64, 512), f32),
            pltpu.VMEM((32, 512), f32),
            pltpu.VMEM((16, 512), f32),
            pltpu.VMEM((16, 512), f32),
            pltpu.VMEM((TERMS, HALF, 128), f32),
            pltpu.VMEM((TERMS, 3 * SHARE[0], 128), f32),
            pltpu.VMEM((TERMS, 3 * SHARE[1], 128), f32),
            pltpu.VMEM((TERMS, 3 * SHARE[2], 128), f32),
            dma((4,)),
            dma((4,)),
            dma((2,)),
            dma((2,)),
            dma((2,)),
            dma((TERMS,)),
            dma((TERMS, 8)),
            dma((TERMS, 8)),
        ],
        compiler_params=pltpu.CompilerParams(
            vmem_limit_bytes=60 << 20, collective_id=0, has_side_effects=True
        ),
    )(
        die_basis,
        die_coeff.reshape(TERMS, 512),
        pkg_basis,
        send_blocks,
        columns,
        counts,
        pkg_blocks,
    )


def solution(mesh):
    placed = (
        P("gx", "gy", None),
        P(None, "gx", "gy"),
        P(("gx", "gy"), None, None),
        P(("gx", "gy"), None, None),
        P(None, ("gx", "gy"), None),
        P(None, ("gx", "gy")),
        P(None, ("gx", "gy"), None, None),
    )
    return jax.shard_map(body, mesh=mesh, in_specs=placed, out_specs=P(), check_vma=False)
```

```python
import jax
import jax.numpy as jnp
from jax import lax
from jax.experimental import pallas as pl
from jax.experimental.pallas import tpu as pltpu
from jax.sharding import PartitionSpec as P

MESH = pl.DeviceIdType.MESH
f32 = jnp.float32
bf16 = jnp.bfloat16
TERMS = 5
UNITS = 2 * TERMS
HALF = 512
SHARE = (128, 32, 8)
TURNS = (0, 1, 3, 4, 5, 6, 7, 9, 10)


def split(value):
    high = value.astype(bf16)
    low = (value - high.astype(f32)).astype(bf16)
    return high, low


def dot3(left, right):
    return jnp.dot(
        jnp.concatenate([left[0], left[1], left[0]], axis=1),
        jnp.concatenate([right[0], right[0], right[1]], axis=0),
        preferred_element_type=f32,
    )


def kernel(
    die, coeff, basis, lists, columns, counts, blocks, summed,
    table, basis_t, staged, image, field_t, field, share,
    ghost_out, ghost_in, row_in, col_out, col_in, got_core, got_0, got_1, got_2,
    ghost_send, ghost_recv, halo_send, halo_recv, stage_sem, send_sem, recv_sem,
):
    gx, gy = lax.axis_index("gx"), lax.axis_index("gy")
    core = lax.rem(gy, 2)
    spot = ((gx // 4) * 2 + lax.rem(gy // 2, 2), gy // 4, lax.rem(gx, 4))
    got = (got_0, got_1, got_2)

    def device_at(x, y, z, on_core):
        return ((x // 2) * 4 + z, y * 4 + lax.rem(x, 2) * 2 + on_core)

    def which(axis):
        return ((2 - axis) * (1 - axis) // 2, axis * (2 - axis), axis * (axis - 1) // 2)

    def along(axis, steps):
        x, y, z = (lax.rem(s + steps * w, 4) for s, w in zip(spot, which(axis)))
        return device_at(x, y, z, core)

    def place_on(axis):
        return sum(s * w for s, w in zip(spot, which(axis)))

    sibling = device_at(*spot, 1 - core)
    around = (
        (lax.rem(gx + 1, 8), gy),
        (lax.rem(gx + 7, 8), gy),
        (gx, lax.rem(gy + 1, 16)),
        (gx, lax.rem(gy + 15, 16)),
    )

    def stage_copy(unit, slot):
        return pltpu.make_async_copy(
            blocks.at[lax.rem(unit, TERMS)], staged.at[slot], stage_sem.at[slot]
        )

    stage_copy(0, 0).start()

    barrier = pltpu.get_barrier_semaphore()
    partners = [along(axis, steps) for axis in range(3) for steps in (1, 2, 3)]
    partners += [sibling, *around]
    for partner in partners:
        pl.semaphore_signal(barrier, inc=1, device_id=partner, device_id_type=MESH)
    pl.semaphore_wait(barrier, len(partners))

    def remote(source, target, send, recv, device):
        return pltpu.make_async_remote_copy(
            src_ref=source, dst_ref=target, send_sem=send, recv_sem=recv,
            device_id=device, device_id_type=MESH,
        )

    row_copy = remote(die.at[0], row_in, halo_send.at[0], halo_recv.at[0], around[1])
    row_copy.start()
    col_out[...] = die[:, 0, :]
    col_copy = remote(col_out, col_in, halo_send.at[1], halo_recv.at[1], around[3])
    col_copy.start()
    ghost_copies = []
    for part in range(2):
        for side in range(4):
            for slot in range(4):
                block = basis[lists[0, side, slot]]
                ghost_out[part, side, slot] = block[:, part * 256 : (part + 1) * 256]
            copy = remote(
                ghost_out.at[part, side], ghost_in.at[part, side],
                ghost_send.at[part, side], ghost_recv.at[part, side], around[side],
            )
            copy.start()
            ghost_copies.append(copy)

    def prepare(group, carry):
        value = basis[pl.ds(group * 4, 4)].reshape(256, 512)
        high, low = split(value)
        for part in range(2):
            lanes = slice(part * 256, (part + 1) * 256)
            table[part, pl.ds(group * 4, 4), :, :256] = high[:, lanes].reshape(4, 64, 256)
            table[part, pl.ds(group * 4, 4), :, 256:] = low[:, lanes].reshape(4, 64, 256)
        high, low = split(value.T)
        basis_t[group, 0] = high
        basis_t[group, 1] = low
        return carry

    lax.fori_loop(0, 8, prepare, 0)

    own = die[...]
    row_copy.wait()
    col_copy.wait()
    next_row = jnp.where(gx == 7, 0.0, row_in[...])
    next_col = jnp.where(gy == 15, 0.0, col_in[...])

    def keep_field(index, value):
        flat = value.reshape(512, 512)
        high, low = split(flat)
        field[index, 0] = high
        field[index, 1] = low
        field_t[index] = flat.T

    keep_field(0, own)
    keep_field(1, own - jnp.concatenate([own[1:], next_row[None]], axis=0))
    last = lax.broadcasted_iota(jnp.int32, (16, 32, 512), 1) == 31
    keep_field(2, own - jnp.where(last, next_col[:, None, :], jnp.roll(own, -1, axis=1)))
    share[...] = jnp.zeros_like(share)

    def die_term(step, carry):
        index = step // 2
        odd = lax.rem(step, 2)
        term = (1 - odd) * index + odd * (3 + (index + 1) // 2)
        fields = coeff[term]
        weights = jnp.concatenate([fields[row : row + 1] for row in range(16)], axis=1)
        weighted = split(field_t[index] * weights)
        gram = dot3(weighted, (field[index, 0], field[index, 1]))
        for lane in range(4):
            here = slice((lane % 2) * 512, (lane % 2 + 1) * 512)
            share[(lane // 2) * TERMS + term, here] += gram[:, lane * 128 : (lane + 1) * 128]
        return carry

    lax.fori_loop(0, 6, die_term, 0)

    def take_ghosts(part):
        for side in range(4):
            ghost_copies[part * 4 + side].wait()
            high, low = split(ghost_in[part, side])
            table[part, 32 + side * 4 : 36 + side * 4, :, :256] = high
            table[part, 32 + side * 4 : 36 + side * 4, :, 256:] = low

    take_ghosts(0)

    lane_at = lax.broadcasted_iota(jnp.int32, (64, 256), 1)

    def compute(unit):
        part, term, slot = unit // TERMS, lax.rem(unit, TERMS), lax.rem(unit, 2)
        stage_copy(unit, slot).wait()

        @pl.when(unit < UNITS - 1)
        def _():
            stage_copy(unit + 1, 1 - slot).start()

        def images(group, carry):
            for step in range(16):
                row = group * 16 + step
                kept = jnp.where(lane_at < counts[term, row] * 64, staged[slot, row], 0.0)
                both = jnp.dot(
                    jnp.concatenate(split(kept), axis=0),
                    jnp.concatenate(
                        [table[part, columns[term, entry, row]] for entry in range(4)], axis=0
                    ),
                    preferred_element_type=f32,
                )
                high, low = split(both[:64, :256] + both[64:, :256] + both[:64, 256:])
                here = pl.ds(pl.multiple_of(row * 64, 64), 64)
                image[0, here] = high
                image[1, here] = low
            return carry

        lax.fori_loop(0, 2, images, 0)
        highs = [basis_t[group, 0] for group in range(8)]
        lows = [basis_t[group, 1] for group in range(8)]
        product = jnp.dot(
            jnp.concatenate(highs + lows + highs, axis=1),
            jnp.concatenate([image[0], image[0], image[1]], axis=0),
            preferred_element_type=f32,
        )
        share[unit, :512] += product[:, :128]
        share[unit, 512:] += product[:, 128:]

    def offset(term, level):
        start = core * HALF
        for i in range(level):
            start = start + place_on(lax.rem(term + i, 3)) * SHARE[i]
        return pl.multiple_of(start, 8)

    def wait_bytes(ref, sem):
        pltpu.make_async_copy(ref, ref, sem).wait()

    def core_send(term):
        there = pl.multiple_of((1 - core) * HALF, 8)
        remote(
            share.at[term, pl.ds(there, HALF)], got_core.at[term],
            send_sem.at[term, 0], recv_sem.at[term, 0], sibling,
        ).start()

    def core_add(term):
        wait_bytes(got_core.at[term], recv_sem.at[term, 0])
        share[term, pl.ds(offset(term, 0), HALF)] += got_core[term]

    def scatter(term, level):
        axis, base, rows = lax.rem(term + level, 3), offset(term, level), SHARE[level]
        for steps in (1, 2, 3):
            there = pl.multiple_of(base + lax.rem(place_on(axis) + steps, 4) * rows, 8)
            remote(
                share.at[term, pl.ds(there, rows)],
                got[level].at[term, pl.ds((steps - 1) * rows, rows)],
                send_sem.at[term, 1 + level], recv_sem.at[term, 1 + level], along(axis, steps),
            ).start()

    def add(term, level, target):
        wait_bytes(got[level].at[term], recv_sem.at[term, 1 + level])
        rows, here = SHARE[level], pl.ds(offset(term, level + 1), SHARE[level])
        target[term, here] = (
            share[term, here]
            + got[level][term, :rows]
            + got[level][term, rows : 2 * rows]
            + got[level][term, 2 * rows :]
        )

    def gather(term, level):
        here = pl.ds(offset(term, level + 1), SHARE[level])
        axis = lax.rem(term + level, 3)
        for steps in (1, 2, 3):
            remote(
                summed.at[term, here], summed.at[term, here],
                send_sem.at[term, 4 + level], recv_sem.at[term, 4 + level], along(axis, steps),
            ).start()

    def gathered(term, level):
        wait_bytes(got[level].at[term], recv_sem.at[term, 4 + level])

    def core_gather(term):
        here = pl.ds(offset(term, 0), HALF)
        remote(
            summed.at[term, here], summed.at[term, here],
            send_sem.at[term, 7], recv_sem.at[term, 7], sibling,
        ).start()

    def close(term):
        wait_bytes(got_core.at[term], recv_sem.at[term, 7])

    def stage_0(term):
        core_send(term)

    def stage_1(term):
        core_add(term)
        scatter(term, 0)

    def stage_2(term):
        add(term, 0, share)
        scatter(term, 1)

    def stage_3(term):
        add(term, 1, share)
        scatter(term, 2)

    def stage_4(term):
        add(term, 2, summed)
        gather(term, 2)

    def stage_5(term):
        gathered(term, 2)
        gather(term, 1)

    def stage_6(term):
        gathered(term, 1)
        gather(term, 0)

    def stage_7(term):
        gathered(term, 0)
        core_gather(term)

    stages = (stage_0, stage_1, stage_2, stage_3, stage_4, stage_5, stage_6, stage_7, close)

    def turn(at, carry):
        @pl.when(at < UNITS)
        def _():
            @pl.when(at == TERMS)
            def _():
                take_ghosts(1)

            compute(at)

        for k in reversed(range(len(stages))):
            unit = at - TURNS[k]

            @pl.when((unit >= 0) & (unit < UNITS))
            def _(k=k, unit=unit):
                stages[k](unit)

        return carry

    lax.fori_loop(0, UNITS + TURNS[-1], turn, 0)

    def finish(term, carry):
        for k in (0, 7):
            wait_bytes(got_core.at[term], send_sem.at[term, k])
        for level in range(3):
            wait_bytes(got[level].at[term], send_sem.at[term, 1 + level])
            wait_bytes(got[level].at[term], send_sem.at[term, 4 + level])
        return carry

    lax.fori_loop(0, UNITS, finish, 0)


def lay_out(summed, out, sem):
    copies = []
    for unit in range(UNITS):
        for slab in range(2):
            column = (unit // TERMS) * 256 + slab * 128
            copies.append(
                pltpu.make_async_copy(
                    summed.at[unit, slab * 512 : (slab + 1) * 512],
                    out.at[unit % TERMS, :, column : column + 128],
                    sem.at[unit, slab],
                )
            )
    for copy in copies:
        copy.start()
    for copy in copies:
        copy.wait()


def body(die_basis, die_coeff, pkg_basis, send_blocks, columns, counts, pkg_blocks):
    vmem = pl.BlockSpec(memory_space=pltpu.VMEM)
    smem = pl.BlockSpec(memory_space=pltpu.SMEM)
    anywhere = pl.BlockSpec(memory_space=pl.ANY)
    dma = pltpu.SemaphoreType.DMA
    summed = pl.pallas_call(
        kernel,
        out_shape=pltpu.VMEM((UNITS, 2 * HALF, 128), f32),
        in_specs=[vmem, vmem, vmem, smem, smem, smem, anywhere],
        out_specs=vmem,
        scratch_shapes=[
            pltpu.VMEM((2, 48, 64, 512), bf16),
            pltpu.VMEM((8, 2, 512, 256), bf16),
            pltpu.VMEM((2, 32, 64, 256), f32),
            pltpu.VMEM((2, 2048, 256), bf16),
            pltpu.VMEM((3, 512, 512), f32),
            pltpu.VMEM((3, 2, 512, 512), bf16),
            pltpu.VMEM((UNITS, 2 * HALF, 128), f32),
            pltpu.VMEM((2, 4, 4, 64, 256), f32),
            pltpu.VMEM((2, 4, 4, 64, 256), f32),
            pltpu.VMEM((32, 512), f32),
            pltpu.VMEM((16, 512), f32),
            pltpu.VMEM((16, 512), f32),
            pltpu.VMEM((UNITS, HALF, 128), f32),
            pltpu.VMEM((UNITS, 3 * SHARE[0], 128), f32),
            pltpu.VMEM((UNITS, 3 * SHARE[1], 128), f32),
            pltpu.VMEM((UNITS, 3 * SHARE[2], 128), f32),
            dma((2, 4)),
            dma((2, 4)),
            dma((2,)),
            dma((2,)),
            dma((2,)),
            dma((UNITS, 8)),
            dma((UNITS, 8)),
        ],
        compiler_params=pltpu.CompilerParams(
            vmem_limit_bytes=56 << 20, collective_id=0, has_side_effects=True
        ),
    )(
        die_basis,
        die_coeff,
        pkg_basis,
        send_blocks,
        jnp.transpose(columns, (0, 2, 1)),
        counts,
        pkg_blocks,
    )
    return pl.pallas_call(
        lay_out,
        out_shape=jax.ShapeDtypeStruct((TERMS, 512, 512), f32),
        in_specs=[anywhere],
        out_specs=anywhere,
        scratch_shapes=[dma((UNITS, 2))],
        compiler_params=pltpu.CompilerParams(vmem_limit_bytes=1 << 20),
    )(summed)


def solution(mesh):
    placed = (
        P("gx", "gy", None),
        P(None, "gx", "gy"),
        P(("gx", "gy"), None, None),
        P(("gx", "gy"), None, None),
        P(None, ("gx", "gy"), None),
        P(None, ("gx", "gy")),
        P(None, ("gx", "gy"), None, None),
    )
    return jax.shard_map(body, mesh=mesh, in_specs=placed, out_specs=P(), check_vma=False)
```

```python
import jax
import jax.numpy as jnp
from jax import lax
from jax.experimental import pallas as pl
from jax.experimental.pallas import tpu as pltpu
from jax.sharding import PartitionSpec as P

MESH = pl.DeviceIdType.MESH
f32 = jnp.float32
bf16 = jnp.bfloat16
TERMS = 5
UNITS = 2 * TERMS
HALF = 512
SHARE = (128, 32, 8)
TURNS = (0, 1, 3, 4, 5, 6, 7, 9, 10)
EARLY = 3
PLANE = 7
OTHERS = [(i, j) for i in range(4) for j in range(4) if (i, j) != (0, 0)]


def split(value):
    high = value.astype(bf16)
    low = (value - high.astype(f32)).astype(bf16)
    return high, low


def dot3(left, right):
    return jnp.dot(
        jnp.concatenate([left[0], left[1], left[0]], axis=1),
        jnp.concatenate([right[0], right[0], right[1]], axis=0),
        preferred_element_type=f32,
    )


def kernel(
    die, coeff, basis, lists, columns, counts, blocks, summed,
    table, basis_t, staged, image, field_t, field, share,
    ghost_out, ghost_in, row_in, col_out, col_in, got_core, got_0, got_1, got_2, got_plane,
    ghost_send, ghost_recv, halo_send, halo_recv, stage_sem, send_sem, recv_sem,
):
    gx, gy = lax.axis_index("gx"), lax.axis_index("gy")
    core = lax.rem(gy, 2)
    spot = ((gx // 4) * 2 + lax.rem(gy // 2, 2), gy // 4, lax.rem(gx, 4))
    got = (got_0, got_1, got_2)

    def device_at(x, y, z, on_core):
        return ((x // 2) * 4 + z, y * 4 + lax.rem(x, 2) * 2 + on_core)

    def which(axis):
        return ((2 - axis) * (1 - axis) // 2, axis * (2 - axis), axis * (axis - 1) // 2)

    def along(axis, steps):
        x, y, z = (lax.rem(s + steps * w, 4) for s, w in zip(spot, which(axis)))
        return device_at(x, y, z, core)

    def place_on(axis):
        return sum(s * w for s, w in zip(spot, which(axis)))

    def across(unit, i, j):
        steps = [0, 0, 0]
        steps[(unit + 1) % 3], steps[(unit + 2) % 3] = i, j
        return device_at(*(lax.rem(s + n, 4) for s, n in zip(spot, steps)), core)

    sibling = device_at(*spot, 1 - core)
    around = (
        (lax.rem(gx + 1, 8), gy),
        (lax.rem(gx + 7, 8), gy),
        (gx, lax.rem(gy + 1, 16)),
        (gx, lax.rem(gy + 15, 16)),
    )

    def stage_copy(unit, slot):
        return pltpu.make_async_copy(
            blocks.at[lax.rem(unit, TERMS)], staged.at[slot], stage_sem.at[slot]
        )

    stage_copy(0, 0).start()

    barrier = pltpu.get_barrier_semaphore()
    partners = [along(axis, steps) for axis in range(3) for steps in (1, 2, 3)]
    for unit in range(PLANE, UNITS):
        partners += [across(unit, i, j) for i, j in OTHERS if i and j]
    partners += [sibling, *around]
    for partner in partners:
        pl.semaphore_signal(barrier, inc=1, device_id=partner, device_id_type=MESH)
    pl.semaphore_wait(barrier, len(partners))

    def remote(source, target, send, recv, device):
        return pltpu.make_async_remote_copy(
            src_ref=source, dst_ref=target, send_sem=send, recv_sem=recv,
            device_id=device, device_id_type=MESH,
        )

    row_copy = remote(die.at[0], row_in, halo_send.at[0], halo_recv.at[0], around[1])
    row_copy.start()
    col_out[...] = die[:, 0, :]
    col_copy = remote(col_out, col_in, halo_send.at[1], halo_recv.at[1], around[3])
    col_copy.start()
    ghost_copies = []
    for part in range(2):
        for side in range(4):
            for slot in range(4):
                block = basis[lists[0, side, slot]]
                ghost_out[part, side, slot] = block[:, part * 256 : (part + 1) * 256]
            copy = remote(
                ghost_out.at[part, side], ghost_in.at[part, side],
                ghost_send.at[part, side], ghost_recv.at[part, side], around[side],
            )
            copy.start()
            ghost_copies.append(copy)

    def prepare(group, carry):
        value = basis[pl.ds(group * 4, 4)].reshape(256, 512)
        high, low = split(value)
        for part in range(2):
            lanes = slice(part * 256, (part + 1) * 256)
            table[part, pl.ds(group * 4, 4), :, :256] = high[:, lanes].reshape(4, 64, 256)
            table[part, pl.ds(group * 4, 4), :, 256:] = low[:, lanes].reshape(4, 64, 256)
        high, low = split(value.T)
        basis_t[group, 0] = high
        basis_t[group, 1] = low
        return carry

    lax.fori_loop(0, 8, prepare, 0)

    own = die[...]
    row_copy.wait()
    col_copy.wait()
    next_row = jnp.where(gx == 7, 0.0, row_in[...])
    next_col = jnp.where(gy == 15, 0.0, col_in[...])

    def keep_field(index, value):
        flat = value.reshape(512, 512)
        high, low = split(flat)
        field[index, 0] = high
        field[index, 1] = low
        field_t[index] = flat.T

    keep_field(0, own)
    keep_field(1, own - jnp.concatenate([own[1:], next_row[None]], axis=0))
    last = lax.broadcasted_iota(jnp.int32, (16, 32, 512), 1) == 31
    keep_field(2, own - jnp.where(last, next_col[:, None, :], jnp.roll(own, -1, axis=1)))
    share[...] = jnp.zeros_like(share)

    def die_term(step, carry):
        index = step // 2
        odd = lax.rem(step, 2)
        term = (1 - odd) * index + odd * (3 + (index + 1) // 2)
        fields = coeff[term]
        weights = jnp.concatenate([fields[row : row + 1] for row in range(16)], axis=1)
        weighted = split(field_t[index] * weights)
        gram = dot3(weighted, (field[index, 0], field[index, 1]))
        for lane in range(4):
            here = slice((lane % 2) * 512, (lane % 2 + 1) * 512)
            share[(lane // 2) * TERMS + term, here] += gram[:, lane * 128 : (lane + 1) * 128]
        return carry

    lax.fori_loop(0, 6, die_term, 0)

    def take_ghosts(part):
        for side in range(4):
            ghost_copies[part * 4 + side].wait()
            high, low = split(ghost_in[part, side])
            table[part, 32 + side * 4 : 36 + side * 4, :, :256] = high
            table[part, 32 + side * 4 : 36 + side * 4, :, 256:] = low

    take_ghosts(0)

    lane_at = lax.broadcasted_iota(jnp.int32, (64, 256), 1)

    def compute(unit):
        part, term, slot = unit // TERMS, lax.rem(unit, TERMS), lax.rem(unit, 2)
        stage_copy(unit, slot).wait()

        @pl.when(unit < UNITS - 1)
        def _():
            stage_copy(unit + 1, 1 - slot).start()

        def images(group, carry):
            for step in range(16):
                row = group * 16 + step
                kept = jnp.where(lane_at < counts[term, row] * 64, staged[slot, row], 0.0)
                both = jnp.dot(
                    jnp.concatenate(split(kept), axis=0),
                    jnp.concatenate(
                        [table[part, columns[term, entry, row]] for entry in range(4)], axis=0
                    ),
                    preferred_element_type=f32,
                )
                high, low = split(both[:64, :256] + both[64:, :256] + both[:64, 256:])
                here = pl.ds(pl.multiple_of(row * 64, 64), 64)
                image[0, here] = high
                image[1, here] = low
            return carry

        lax.fori_loop(0, 2, images, 0)
        highs = [basis_t[group, 0] for group in range(8)]
        lows = [basis_t[group, 1] for group in range(8)]
        product = jnp.dot(
            jnp.concatenate(highs + lows + highs, axis=1),
            jnp.concatenate([image[0], image[0], image[1]], axis=0),
            preferred_element_type=f32,
        )
        share[unit, :512] += product[:, :128]
        share[unit, 512:] += product[:, 128:]

    def offset(term, level):
        start = core * HALF
        for i in range(level):
            start = start + place_on(lax.rem(term + i, 3)) * SHARE[i]
        return pl.multiple_of(start, 8)

    def wait_bytes(ref, sem):
        pltpu.make_async_copy(ref, ref, sem).wait()

    def core_send(term):
        there = pl.multiple_of((1 - core) * HALF, 8)
        remote(
            share.at[term, pl.ds(there, HALF)], got_core.at[term],
            send_sem.at[term, 0], recv_sem.at[term, 0], sibling,
        ).start()

    def core_add(term):
        wait_bytes(got_core.at[term], recv_sem.at[term, 0])
        share[term, pl.ds(offset(term, 0), HALF)] += got_core[term]

    def scatter(term, level):
        axis, base, rows = lax.rem(term + level, 3), offset(term, level), SHARE[level]
        for steps in (1, 2, 3):
            there = pl.multiple_of(base + lax.rem(place_on(axis) + steps, 4) * rows, 8)
            remote(
                share.at[term, pl.ds(there, rows)],
                got[level].at[term, pl.ds((steps - 1) * rows, rows)],
                send_sem.at[term, 1 + level], recv_sem.at[term, 1 + level], along(axis, steps),
            ).start()

    def add(term, level, target):
        wait_bytes(got[level].at[term], recv_sem.at[term, 1 + level])
        rows, here = SHARE[level], pl.ds(offset(term, level + 1), SHARE[level])
        target[term, here] = (
            share[term, here]
            + got[level][term, :rows]
            + got[level][term, rows : 2 * rows]
            + got[level][term, 2 * rows :]
        )

    def gather(term, level):
        here = pl.ds(offset(term, level + 1), SHARE[level])
        axis = lax.rem(term + level, 3)
        for steps in (1, 2, 3):
            remote(
                summed.at[term, here], summed.at[term, here],
                send_sem.at[term, 4 + level], recv_sem.at[term, 4 + level], along(axis, steps),
            ).start()

    def gathered(term, level):
        wait_bytes(got[level].at[term], recv_sem.at[term, 4 + level])

    def core_gather(term):
        here = pl.ds(offset(term, 0), HALF)
        remote(
            summed.at[term, here], summed.at[term, here],
            send_sem.at[term, 7], recv_sem.at[term, 7], sibling,
        ).start()

    def close(term):
        wait_bytes(got_core.at[term], recv_sem.at[term, 7])

    def stage_0(term):
        core_send(term)

    def stage_1(term):
        core_add(term)
        scatter(term, 0)

    def stage_2(term):
        add(term, 0, share)
        scatter(term, 1)

    def stage_3(term):
        add(term, 1, share)
        scatter(term, 2)

    def stage_4(term):
        add(term, 2, summed)
        gather(term, 2)

    def stage_5(term):
        gathered(term, 2)
        gather(term, 1)

    def stage_6(term):
        gathered(term, 1)
        gather(term, 0)

    def stage_7(term):
        gathered(term, 0)
        core_gather(term)

    stages = (stage_0, stage_1, stage_2, stage_3, stage_4, stage_5, stage_6, stage_7, close)

    def plane_scatter(unit):
        add(unit, 0, share)
        base = offset(unit, 1)
        first, second = spot[(unit + 1) % 3], spot[(unit + 2) % 3]
        for slot, (i, j) in enumerate(OTHERS):
            there = base + lax.rem(first + i, 4) * 32 + lax.rem(second + j, 4) * 8
            remote(
                share.at[unit, pl.ds(pl.multiple_of(there, 8), 8)],
                got_plane.at[unit - PLANE, pl.ds(slot * 8, 8)],
                send_sem.at[unit, 2], recv_sem.at[unit, 2], across(unit, i, j),
            ).start()

    def plane_gather(unit):
        wait_bytes(got_plane.at[unit - PLANE], recv_sem.at[unit, 2])
        here = pl.ds(offset(unit, 3), 8)
        tile = share[unit, here]
        for slot in range(15):
            tile = tile + got_plane[unit - PLANE, slot * 8 : (slot + 1) * 8]
        summed[unit, here] = tile
        for i, j in OTHERS:
            remote(
                summed.at[unit, here], summed.at[unit, here],
                send_sem.at[unit, 5], recv_sem.at[unit, 5], across(unit, i, j),
            ).start()

    def plane_gathered(unit):
        wait_bytes(got_plane.at[unit - PLANE], recv_sem.at[unit, 5])
        gather(unit, 0)

    short = (stage_0, stage_1, plane_scatter, plane_gather, plane_gathered, stage_7, close)

    def turn(at, carry):
        @pl.when(at == TERMS)
        def _():
            take_ghosts(1)

        compute(at)
        for k in reversed(range(len(stages))):
            if k < EARLY:
                unit = at - TURNS[k]
                last = UNITS if k < 2 else PLANE

                @pl.when((unit >= 0) & (unit < last))
                def _(k=k, unit=unit):
                    stages[k](unit)

        return carry

    lax.fori_loop(0, UNITS, turn, 0)

    left = {}
    for unit in range(UNITS):
        steps = stages if unit < PLANE else short
        at = 0
        for k, stage in enumerate(steps):
            in_loop = k < EARLY and unit + TURNS[k] < UNITS and (k < 2 or unit < PLANE)
            at = unit + TURNS[k] if in_loop else max(at + 1, UNITS)
            if stage in (stage_7, close):
                at = max(at, 2 * UNITS)
            if not in_loop:
                left.setdefault(at, []).append((k, unit, stage))
    for at in sorted(left):
        for k, unit, stage in sorted(left[at], key=lambda entry: entry[1]):
            stage(unit)

    def finish(term, carry):
        for k in (0, 7):
            wait_bytes(got_core.at[term], send_sem.at[term, k])
        for level in range(3):
            wait_bytes(got[level].at[term], send_sem.at[term, 1 + level])
            wait_bytes(got[level].at[term], send_sem.at[term, 4 + level])
        return carry

    lax.fori_loop(0, PLANE, finish, 0)
    for unit in range(PLANE, UNITS):
        for k in (0, 7):
            wait_bytes(got_core.at[unit], send_sem.at[unit, k])
        for k in (1, 4):
            wait_bytes(got_0.at[unit], send_sem.at[unit, k])
        for k in (2, 5):
            wait_bytes(got_plane.at[unit - PLANE], send_sem.at[unit, k])


def lay_out(summed, out, sem):
    copies = []
    for unit in range(UNITS):
        for slab in range(2):
            column = (unit // TERMS) * 256 + slab * 128
            copies.append(
                pltpu.make_async_copy(
                    summed.at[unit, slab * 512 : (slab + 1) * 512],
                    out.at[unit % TERMS, :, column : column + 128],
                    sem.at[unit, slab],
                )
            )
    for copy in copies:
        copy.start()
    for copy in copies:
        copy.wait()


def body(die_basis, die_coeff, pkg_basis, send_blocks, columns, counts, pkg_blocks):
    vmem = pl.BlockSpec(memory_space=pltpu.VMEM)
    smem = pl.BlockSpec(memory_space=pltpu.SMEM)
    anywhere = pl.BlockSpec(memory_space=pl.ANY)
    dma = pltpu.SemaphoreType.DMA
    summed = pl.pallas_call(
        kernel,
        out_shape=pltpu.VMEM((UNITS, 2 * HALF, 128), f32),
        in_specs=[vmem, vmem, vmem, smem, smem, smem, anywhere],
        out_specs=vmem,
        scratch_shapes=[
            pltpu.VMEM((2, 48, 64, 512), bf16),
            pltpu.VMEM((8, 2, 512, 256), bf16),
            pltpu.VMEM((2, 32, 64, 256), f32),
            pltpu.VMEM((2, 2048, 256), bf16),
            pltpu.VMEM((3, 512, 512), f32),
            pltpu.VMEM((3, 2, 512, 512), bf16),
            pltpu.VMEM((UNITS, 2 * HALF, 128), f32),
            pltpu.VMEM((2, 4, 4, 64, 256), f32),
            pltpu.VMEM((2, 4, 4, 64, 256), f32),
            pltpu.VMEM((32, 512), f32),
            pltpu.VMEM((16, 512), f32),
            pltpu.VMEM((16, 512), f32),
            pltpu.VMEM((UNITS, HALF, 128), f32),
            pltpu.VMEM((UNITS, 3 * SHARE[0], 128), f32),
            pltpu.VMEM((UNITS, 3 * SHARE[1], 128), f32),
            pltpu.VMEM((UNITS, 3 * SHARE[2], 128), f32),
            pltpu.VMEM((UNITS - PLANE, 120, 128), f32),
            dma((2, 4)),
            dma((2, 4)),
            dma((2,)),
            dma((2,)),
            dma((2,)),
            dma((UNITS, 8)),
            dma((UNITS, 8)),
        ],
        compiler_params=pltpu.CompilerParams(
            vmem_limit_bytes=56 << 20, collective_id=0, has_side_effects=True
        ),
    )(
        die_basis,
        die_coeff,
        pkg_basis,
        send_blocks,
        jnp.transpose(columns, (0, 2, 1)),
        counts,
        pkg_blocks,
    )
    return pl.pallas_call(
        lay_out,
        out_shape=jax.ShapeDtypeStruct((TERMS, 512, 512), f32),
        in_specs=[anywhere],
        out_specs=anywhere,
        scratch_shapes=[dma((UNITS, 2))],
        compiler_params=pltpu.CompilerParams(vmem_limit_bytes=1 << 20),
    )(summed)


def solution(mesh):
    placed = (
        P("gx", "gy", None),
        P(None, "gx", "gy"),
        P(("gx", "gy"), None, None),
        P(("gx", "gy"), None, None),
        P(None, ("gx", "gy"), None),
        P(None, ("gx", "gy")),
        P(None, ("gx", "gy"), None, None),
    )
    return jax.shard_map(body, mesh=mesh, in_specs=placed, out_specs=P(), check_vma=False)
```

```python
import jax
import jax.numpy as jnp
from jax import lax
from jax.experimental import pallas as pl
from jax.experimental.pallas import tpu as pltpu
from jax.sharding import PartitionSpec as P

MESH = pl.DeviceIdType.MESH
f32 = jnp.float32
bf16 = jnp.bfloat16
TERMS = 5
UNITS = 2 * TERMS
HALF = 512
SHARE = (128, 32, 8)
TURNS = (0, 1, 3, 4, 5, 6, 7, 9, 10)
EARLY = 3
PLANE = 7
OTHERS = [(i, j) for i in range(4) for j in range(4) if (i, j) != (0, 0)]


def split(value):
    high = value.astype(bf16)
    low = (value - high.astype(f32)).astype(bf16)
    return high, low


def dot3(left, right):
    return jnp.dot(
        jnp.concatenate([left[0], left[1], left[0]], axis=1),
        jnp.concatenate([right[0], right[0], right[1]], axis=0),
        preferred_element_type=f32,
    )


def kernel(
    die, coeff, basis, lists, columns, counts, blocks, summed,
    table, basis_t, staged, image, field_t, field, share,
    ghost_out, ghost_in, row_in, col_out, col_in, got_core, got_0, got_1, got_2, got_plane,
    ghost_send, ghost_recv, halo_send, halo_recv, stage_sem, send_sem, recv_sem,
):
    gx, gy = lax.axis_index("gx"), lax.axis_index("gy")
    core = lax.rem(gy, 2)
    spot = ((gx // 4) * 2 + lax.rem(gy // 2, 2), gy // 4, lax.rem(gx, 4))
    got = (got_0, got_1, got_2)

    def device_at(x, y, z, on_core):
        return ((x // 2) * 4 + z, y * 4 + lax.rem(x, 2) * 2 + on_core)

    def which(axis):
        return ((2 - axis) * (1 - axis) // 2, axis * (2 - axis), axis * (axis - 1) // 2)

    def along(axis, steps):
        x, y, z = (lax.rem(s + steps * w, 4) for s, w in zip(spot, which(axis)))
        return device_at(x, y, z, core)

    def place_on(axis):
        return sum(s * w for s, w in zip(spot, which(axis)))

    def across(unit, i, j):
        steps = [0, 0, 0]
        steps[(unit + 1) % 3], steps[(unit + 2) % 3] = i, j
        return device_at(*(lax.rem(s + n, 4) for s, n in zip(spot, steps)), core)

    sibling = device_at(*spot, 1 - core)
    around = (
        (lax.rem(gx + 1, 8), gy),
        (lax.rem(gx + 7, 8), gy),
        (gx, lax.rem(gy + 1, 16)),
        (gx, lax.rem(gy + 15, 16)),
    )

    def stage_copy(unit, slot):
        return pltpu.make_async_copy(
            blocks.at[lax.rem(unit, TERMS)], staged.at[slot], stage_sem.at[slot]
        )

    stage_copy(0, 0).start()

    barrier = pltpu.get_barrier_semaphore()
    partners = [along(axis, steps) for axis in range(3) for steps in (1, 2, 3)]
    for unit in range(PLANE, UNITS):
        partners += [across(unit, i, j) for i, j in OTHERS if i and j]
    partners += [sibling, *around]
    for partner in partners:
        pl.semaphore_signal(barrier, inc=1, device_id=partner, device_id_type=MESH)
    pl.semaphore_wait(barrier, len(partners))

    def remote(source, target, send, recv, device):
        return pltpu.make_async_remote_copy(
            src_ref=source, dst_ref=target, send_sem=send, recv_sem=recv,
            device_id=device, device_id_type=MESH,
        )

    row_copy = remote(die.at[0], row_in, halo_send.at[0], halo_recv.at[0], around[1])
    row_copy.start()
    col_out[...] = die[:, 0, :]
    col_copy = remote(col_out, col_in, halo_send.at[1], halo_recv.at[1], around[3])
    col_copy.start()
    ghost_copies = []
    for part in range(2):
        for side in range(4):
            for slot in range(4):
                block = basis[lists[0, side, slot]]
                ghost_out[part, side, slot] = block[:, part * 256 : (part + 1) * 256]
            copy = remote(
                ghost_out.at[part, side], ghost_in.at[part, side],
                ghost_send.at[part, side], ghost_recv.at[part, side], around[side],
            )
            copy.start()
            ghost_copies.append(copy)

    def prepare(group, carry):
        value = basis[pl.ds(group * 4, 4)].reshape(256, 512)
        high, low = split(value)
        for part in range(2):
            lanes = slice(part * 256, (part + 1) * 256)
            table[part, pl.ds(group * 4, 4), :, :256] = high[:, lanes].reshape(4, 64, 256)
            table[part, pl.ds(group * 4, 4), :, 256:] = low[:, lanes].reshape(4, 64, 256)
        high, low = split(value.T)
        basis_t[group, 0] = high
        basis_t[group, 1] = low
        return carry

    lax.fori_loop(0, 8, prepare, 0)

    own = die[...]
    row_copy.wait()
    col_copy.wait()
    next_row = jnp.where(gx == 7, 0.0, row_in[...])
    next_col = jnp.where(gy == 15, 0.0, col_in[...])

    def keep_field(index, value):
        flat = value.reshape(512, 512)
        high, low = split(flat)
        field[index, 0] = high
        field[index, 1] = low
        field_t[index] = flat.T

    keep_field(0, own)
    keep_field(1, own - jnp.concatenate([own[1:], next_row[None]], axis=0))
    last = lax.broadcasted_iota(jnp.int32, (16, 32, 512), 1) == 31
    keep_field(2, own - jnp.where(last, next_col[:, None, :], jnp.roll(own, -1, axis=1)))
    share[...] = jnp.zeros_like(share)

    def die_term(step, carry):
        index = step // 2
        odd = lax.rem(step, 2)
        term = (1 - odd) * index + odd * (3 + (index + 1) // 2)
        fields = coeff[term]
        weights = jnp.concatenate([fields[row : row + 1] for row in range(16)], axis=1)
        weighted = split(field_t[index] * weights)
        gram = dot3(weighted, (field[index, 0], field[index, 1]))
        for lane in range(4):
            here = slice((lane % 2) * 512, (lane % 2 + 1) * 512)
            share[(lane // 2) * TERMS + term, here] += gram[:, lane * 128 : (lane + 1) * 128]
        return carry

    lax.fori_loop(0, 6, die_term, 0)

    def take_ghosts(part):
        for side in range(4):
            ghost_copies[part * 4 + side].wait()
            high, low = split(ghost_in[part, side])
            table[part, 32 + side * 4 : 36 + side * 4, :, :256] = high
            table[part, 32 + side * 4 : 36 + side * 4, :, 256:] = low

    take_ghosts(0)

    lane_at = lax.broadcasted_iota(jnp.int32, (64, 256), 1)

    def compute(unit):
        part, term, slot = unit // TERMS, lax.rem(unit, TERMS), lax.rem(unit, 2)
        stage_copy(unit, slot).wait()

        @pl.when(unit < UNITS - 1)
        def _():
            stage_copy(unit + 1, 1 - slot).start()

        for row in range(32):
            kept = jnp.where(lane_at < counts[term, row] * 64, staged[slot, row], 0.0)
            both = jnp.dot(
                jnp.concatenate(split(kept), axis=0),
                jnp.concatenate(
                    [table[part, columns[term, entry, row]] for entry in range(4)], axis=0
                ),
                preferred_element_type=f32,
            )
            high, low = split(both[:64, :256] + both[64:, :256] + both[:64, 256:])
            here = slice(row * 64, (row + 1) * 64)
            image[0, here] = high
            image[1, here] = low
        highs = [basis_t[group, 0] for group in range(8)]
        lows = [basis_t[group, 1] for group in range(8)]
        product = jnp.dot(
            jnp.concatenate(highs + lows + highs, axis=1),
            jnp.concatenate([image[0], image[0], image[1]], axis=0),
            preferred_element_type=f32,
        )
        share[unit, :512] += product[:, :128]
        share[unit, 512:] += product[:, 128:]

    def offset(term, level):
        start = core * HALF
        for i in range(level):
            start = start + place_on(lax.rem(term + i, 3)) * SHARE[i]
        return pl.multiple_of(start, 8)

    def wait_bytes(ref, sem):
        pltpu.make_async_copy(ref, ref, sem).wait()

    def core_send(term):
        there = pl.multiple_of((1 - core) * HALF, 8)
        remote(
            share.at[term, pl.ds(there, HALF)], got_core.at[term],
            send_sem.at[term, 0], recv_sem.at[term, 0], sibling,
        ).start()

    def core_add(term):
        wait_bytes(got_core.at[term], recv_sem.at[term, 0])
        share[term, pl.ds(offset(term, 0), HALF)] += got_core[term]

    def scatter(term, level):
        axis, base, rows = lax.rem(term + level, 3), offset(term, level), SHARE[level]
        for steps in (1, 2, 3):
            there = pl.multiple_of(base + lax.rem(place_on(axis) + steps, 4) * rows, 8)
            remote(
                share.at[term, pl.ds(there, rows)],
                got[level].at[term, pl.ds((steps - 1) * rows, rows)],
                send_sem.at[term, 1 + level], recv_sem.at[term, 1 + level], along(axis, steps),
            ).start()

    def add(term, level, target):
        wait_bytes(got[level].at[term], recv_sem.at[term, 1 + level])
        rows, here = SHARE[level], pl.ds(offset(term, level + 1), SHARE[level])
        target[term, here] = (
            share[term, here]
            + got[level][term, :rows]
            + got[level][term, rows : 2 * rows]
            + got[level][term, 2 * rows :]
        )

    def gather(term, level):
        here = pl.ds(offset(term, level + 1), SHARE[level])
        axis = lax.rem(term + level, 3)
        for steps in (1, 2, 3):
            remote(
                summed.at[term, here], summed.at[term, here],
                send_sem.at[term, 4 + level], recv_sem.at[term, 4 + level], along(axis, steps),
            ).start()

    def gathered(term, level):
        wait_bytes(got[level].at[term], recv_sem.at[term, 4 + level])

    def core_gather(term):
        here = pl.ds(offset(term, 0), HALF)
        remote(
            summed.at[term, here], summed.at[term, here],
            send_sem.at[term, 7], recv_sem.at[term, 7], sibling,
        ).start()

    def close(term):
        wait_bytes(got_core.at[term], recv_sem.at[term, 7])

    def stage_0(term):
        core_send(term)

    def stage_1(term):
        core_add(term)
        scatter(term, 0)

    def stage_2(term):
        add(term, 0, share)
        scatter(term, 1)

    def stage_3(term):
        add(term, 1, share)
        scatter(term, 2)

    def stage_4(term):
        add(term, 2, summed)
        gather(term, 2)

    def stage_5(term):
        gathered(term, 2)
        gather(term, 1)

    def stage_6(term):
        gathered(term, 1)
        gather(term, 0)

    def stage_7(term):
        gathered(term, 0)
        core_gather(term)

    stages = (stage_0, stage_1, stage_2, stage_3, stage_4, stage_5, stage_6, stage_7, close)

    def plane_scatter(unit):
        add(unit, 0, share)
        base = offset(unit, 1)
        first, second = spot[(unit + 1) % 3], spot[(unit + 2) % 3]
        for slot, (i, j) in enumerate(OTHERS):
            there = base + lax.rem(first + i, 4) * 32 + lax.rem(second + j, 4) * 8
            remote(
                share.at[unit, pl.ds(pl.multiple_of(there, 8), 8)],
                got_plane.at[unit - PLANE, pl.ds(slot * 8, 8)],
                send_sem.at[unit, 2], recv_sem.at[unit, 2], across(unit, i, j),
            ).start()

    def plane_gather(unit):
        wait_bytes(got_plane.at[unit - PLANE], recv_sem.at[unit, 2])
        here = pl.ds(offset(unit, 3), 8)
        tile = share[unit, here]
        for slot in range(15):
            tile = tile + got_plane[unit - PLANE, slot * 8 : (slot + 1) * 8]
        summed[unit, here] = tile
        for i, j in OTHERS:
            remote(
                summed.at[unit, here], summed.at[unit, here],
                send_sem.at[unit, 5], recv_sem.at[unit, 5], across(unit, i, j),
            ).start()

    def plane_gathered(unit):
        wait_bytes(got_plane.at[unit - PLANE], recv_sem.at[unit, 5])
        gather(unit, 0)

    short = (stage_0, stage_1, plane_scatter, plane_gather, plane_gathered, stage_7, close)

    def turn(at, carry):
        @pl.when(at == TERMS)
        def _():
            take_ghosts(1)

        compute(at)
        for k in reversed(range(len(stages))):
            if k < EARLY:
                unit = at - TURNS[k]
                last = UNITS if k < 2 else PLANE

                @pl.when((unit >= 0) & (unit < last))
                def _(k=k, unit=unit):
                    stages[k](unit)

        return carry

    lax.fori_loop(0, UNITS, turn, 0)

    left = {}
    for unit in range(UNITS):
        steps = stages if unit < PLANE else short
        at = 0
        for k, stage in enumerate(steps):
            in_loop = k < EARLY and unit + TURNS[k] < UNITS and (k < 2 or unit < PLANE)
            at = unit + TURNS[k] if in_loop else max(at + 1, UNITS)
            if stage in (stage_7, close):
                at = max(at, 2 * UNITS)
            if not in_loop:
                left.setdefault(at, []).append((k, unit, stage))
    for at in sorted(left):
        for k, unit, stage in sorted(left[at], key=lambda entry: entry[1]):
            stage(unit)

    def finish(term, carry):
        for k in (0, 7):
            wait_bytes(got_core.at[term], send_sem.at[term, k])
        for level in range(3):
            wait_bytes(got[level].at[term], send_sem.at[term, 1 + level])
            wait_bytes(got[level].at[term], send_sem.at[term, 4 + level])
        return carry

    lax.fori_loop(0, PLANE, finish, 0)
    for unit in range(PLANE, UNITS):
        for k in (0, 7):
            wait_bytes(got_core.at[unit], send_sem.at[unit, k])
        for k in (1, 4):
            wait_bytes(got_0.at[unit], send_sem.at[unit, k])
        for k in (2, 5):
            wait_bytes(got_plane.at[unit - PLANE], send_sem.at[unit, k])


def lay_out(summed, out, sem):
    copies = []
    for unit in range(UNITS):
        for slab in range(2):
            column = (unit // TERMS) * 256 + slab * 128
            copies.append(
                pltpu.make_async_copy(
                    summed.at[unit, slab * 512 : (slab + 1) * 512],
                    out.at[unit % TERMS, :, column : column + 128],
                    sem.at[unit, slab],
                )
            )
    for copy in copies:
        copy.start()
    for copy in copies:
        copy.wait()


def body(die_basis, die_coeff, pkg_basis, send_blocks, columns, counts, pkg_blocks):
    vmem = pl.BlockSpec(memory_space=pltpu.VMEM)
    smem = pl.BlockSpec(memory_space=pltpu.SMEM)
    anywhere = pl.BlockSpec(memory_space=pl.ANY)
    dma = pltpu.SemaphoreType.DMA
    summed = pl.pallas_call(
        kernel,
        out_shape=pltpu.VMEM((UNITS, 2 * HALF, 128), f32),
        in_specs=[vmem, vmem, vmem, smem, smem, smem, anywhere],
        out_specs=vmem,
        scratch_shapes=[
            pltpu.VMEM((2, 48, 64, 512), bf16),
            pltpu.VMEM((8, 2, 512, 256), bf16),
            pltpu.VMEM((2, 32, 64, 256), f32),
            pltpu.VMEM((2, 2048, 256), bf16),
            pltpu.VMEM((3, 512, 512), f32),
            pltpu.VMEM((3, 2, 512, 512), bf16),
            pltpu.VMEM((UNITS, 2 * HALF, 128), f32),
            pltpu.VMEM((2, 4, 4, 64, 256), f32),
            pltpu.VMEM((2, 4, 4, 64, 256), f32),
            pltpu.VMEM((32, 512), f32),
            pltpu.VMEM((16, 512), f32),
            pltpu.VMEM((16, 512), f32),
            pltpu.VMEM((UNITS, HALF, 128), f32),
            pltpu.VMEM((UNITS, 3 * SHARE[0], 128), f32),
            pltpu.VMEM((UNITS, 3 * SHARE[1], 128), f32),
            pltpu.VMEM((UNITS, 3 * SHARE[2], 128), f32),
            pltpu.VMEM((UNITS - PLANE, 120, 128), f32),
            dma((2, 4)),
            dma((2, 4)),
            dma((2,)),
            dma((2,)),
            dma((2,)),
            dma((UNITS, 8)),
            dma((UNITS, 8)),
        ],
        compiler_params=pltpu.CompilerParams(
            vmem_limit_bytes=56 << 20, collective_id=0, has_side_effects=True
        ),
    )(
        die_basis,
        die_coeff,
        pkg_basis,
        send_blocks,
        jnp.transpose(columns, (0, 2, 1)),
        counts,
        pkg_blocks,
    )
    return pl.pallas_call(
        lay_out,
        out_shape=jax.ShapeDtypeStruct((TERMS, 512, 512), f32),
        in_specs=[anywhere],
        out_specs=anywhere,
        scratch_shapes=[dma((UNITS, 2))],
        compiler_params=pltpu.CompilerParams(vmem_limit_bytes=1 << 20),
    )(summed)


def solution(mesh):
    placed = (
        P("gx", "gy", None),
        P(None, "gx", "gy"),
        P(("gx", "gy"), None, None),
        P(("gx", "gy"), None, None),
        P(None, ("gx", "gy"), None),
        P(None, ("gx", "gy")),
        P(None, ("gx", "gy"), None, None),
    )
    return jax.shard_map(body, mesh=mesh, in_specs=placed, out_specs=P(), check_vma=False)
```
